32 devices in a mesh: vertex: 8 (over z, core), tm: 4 (over y, x).
Axes of the slice: x: 2, y: 2, z: 4, core: 2. Of those that a mesh axis runs over, the one named last changes fastest.
Arguments:
- features: bfloat16 [4, 8192, 512], P('tm', 'vertex'), may hold values from -6 to 6
- tile_coord: int32 [4, 1024, 2], P('tm', 'vertex'), may hold values from 0 to 63, as said below
- tile_count: int32 [4, 8], P('tm', 'vertex'), may hold values from 1 to 128, as said below
- tile_values: bfloat16 [4, 1024, 128, 128], P('tm', 'vertex'), may hold values from -0.125 to 0.125
- w_agg: bfloat16 [512, 512], replicated, may hold values from -0.25 to 0.25
- w_root: bfloat16 [512, 512], replicated, may hold values from -0.25 to 0.25
- time_embed: bfloat16 [4, 512], replicated, may hold values from -6 to 6
- gain_first: bfloat16 [512], replicated, may hold values from 0.25 to 1.75
- w_qkv: bfloat16 [512, 1536], replicated, may hold values from -12 to 12
- w_out: bfloat16 [512, 512], replicated, may hold values from -0.25 to 0.25
- gain_second: bfloat16 [512], replicated, may hold values from 0.25 to 1.75
- w_up: bfloat16 [512, 1024], replicated, may hold values from -0.25 to 0.25
- w_down: bfloat16 [1024, 512], replicated, may hold values from -0.1875 to 0.1875
Outputs:
- layer_out: bfloat16 [4, 8192, 512], P(None, ('vertex', 'tm'))
The draws below stay inside these ranges and needn't reach their ends.
Inputs may be any that keep to these rules, and one draw needn't show every extreme that they name: `tile_coord`: entry 0 of a slot is a row block 0 to 7 of the device's own vertices, entry 1 a column block 0 to 63; no pair repeats among one device's 128 slots, live or not. `tile_count`: live slots are the first ones of a device; in every snapshot some device has all 128 slots live.
All inputs are finite; a program needn't handle non-finite values.
Results may differ from the reference program's by a relative error of at most 0.006.
Values may be sent and summed in bfloat16 or wider, within the bound.
A program may use at most 192 MiB of HBM per device.

```python
import math
import jax
import jax.numpy as jnp
from jax import lax

D = 512
HID = 1024
HEADS = 8
TILE = 128
TILE_ROW = 16
VB = 1024
TILES_DEV = 128
NV = 8192
SNAPS = 4
N_VERTEX = 8


def draw_tile_coord(key, part):
    group_count = NV // VB
    row_blocks = VB // TILE
    col_blocks = NV // TILE
    device_keys = jax.random.split(key, SNAPS * group_count)

    def one_device(device_key):
        shuffled = jax.random.permutation(device_key, row_blocks * col_blocks)[:TILES_DEV]
        return jnp.stack([shuffled // col_blocks, shuffled % col_blocks], axis=-1)
    pair_rows = jax.vmap(one_device)(device_keys)
    return pair_rows.reshape(SNAPS, group_count * TILES_DEV, 2).astype(jnp.int32)


def draw_tile_count(key, part):
    group_count = NV // VB
    key_first, key_second = jax.random.split(jax.random.fold_in(key, 7))
    counts = jax.random.randint(key_first, (SNAPS, group_count), 1, TILES_DEV + 1)
    full_index = jax.random.randint(key_second, (SNAPS, 1), 0, group_count)
    filled = jnp.where(jnp.arange(group_count)[None, :] == full_index, TILES_DEV, counts)
    return filled.astype(jnp.int32)


def draw_w_qkv(key, part):
    key_first = jax.random.fold_in(jax.random.fold_in(key, 11), 0)
    base = jax.random.normal(key_first, (D, 3 * D), jnp.float32) / math.sqrt(D)
    return base.astype(jnp.bfloat16)


def shard_levels(stream_key, shape, shards, smallest, high):
    loudness = 1.0
    for axis_at, parts in shards:
        heights = jax.random.uniform(jax.random.fold_in(jax.random.fold_in(stream_key, 6), axis_at), (parts,), jnp.float32, smallest / len(shards), high / len(shards))
        loudness = loudness * jnp.repeat(jnp.exp(heights), shape[axis_at] // parts).reshape((-1,) + (1,) * (len(shape) - 1 - axis_at))
    return loudness


def scatter_about(key, dims, deviation, bound, cuts=(), dtype=jnp.bfloat16):
    factor_of = shard_levels(key, dims, cuts, -0.22, 0.18) if cuts else 1.0
    array = jax.random.normal(key, dims, jnp.float32) * deviation * factor_of
    return jnp.minimum(jnp.maximum(array, -bound), bound).astype(dtype)


def setup_inputs(seed: int = 0) -> dict:
    splits = jax.random.split(jax.random.key(seed), 14)
    features = scatter_about(splits[0], (SNAPS, NV, D), 1.0, 6.0, ((0, 4), (1, 8)))
    tile_coord = draw_tile_coord(jax.random.fold_in(splits[13], 71), 0)
    tile_count = draw_tile_count(jax.random.fold_in(splits[13], 71), 0)
    tile_values = scatter_about(splits[3], (SNAPS, N_VERTEX * TILES_DEV, TILE, TILE), (TILE * TILE_ROW) ** -0.5, 0.125, ((0, 4), (1, 8)))
    w_agg = scatter_about(splits[4], (D, D), D ** -0.5, 0.25)
    w_root = scatter_about(splits[5], (D, D), D ** -0.5, 0.25)
    time_embed = scatter_about(splits[6], (SNAPS, D), 1.0, 6.0)
    gain_first = jnp.clip(1.0 + 0.15 * jax.random.normal(splits[7], (D,), jnp.float32), 0.25, 1.75).astype(jnp.bfloat16)
    w_qkv = draw_w_qkv(jax.random.fold_in(splits[13], 71), 0)
    w_out = scatter_about(splits[9], (D, D), D ** -0.5, 0.25)
    gain_second = jnp.clip(1.0 + 0.15 * jax.random.normal(splits[10], (D,), jnp.float32), 0.25, 1.75).astype(jnp.bfloat16)
    w_up = scatter_about(splits[11], (D, HID), D ** -0.5, 0.25)
    w_down = scatter_about(splits[12], (HID, D), HID ** -0.5, 0.1875)
    return dict(features=features, tile_coord=tile_coord, tile_count=tile_count, tile_values=tile_values, w_agg=w_agg, w_root=w_root, time_embed=time_embed, gain_first=gain_first, w_qkv=w_qkv, w_out=w_out, gain_second=gain_second, w_up=w_up, w_down=w_down)


def norm_rows(values, gain):
    scale = lax.rsqrt(lax.optimization_barrier(jnp.mean(values * values, axis=-1, keepdims=True)) + 1e-06)
    return values * scale * gain.astype(jnp.float32)

def project(left, right):
    return jnp.einsum('sid,de->sie', left.astype(jnp.float32), right.astype(jnp.float32))

def temporal(graph_rows, time_embed, gain_first, w_qkv, w_out, gain_second, w_up, w_down):
    snap_count, item_count, width = graph_rows.shape
    head_size = width // HEADS
    mixed = graph_rows.astype(jnp.float32) + time_embed.astype(jnp.float32)[:, None, :]
    normed = norm_rows(mixed, gain_first).astype(jnp.bfloat16)
    qkv = project(normed, w_qkv).astype(jnp.bfloat16)
    query = qkv[..., :width].reshape(snap_count, item_count, HEADS, head_size).astype(jnp.float32)
    key_rows = qkv[..., width:2 * width].reshape(snap_count, item_count, HEADS, head_size).astype(jnp.float32)
    value_rows = qkv[..., 2 * width:].reshape(snap_count, item_count, HEADS, head_size).astype(jnp.float32)
    scores = jnp.einsum('sihd,tihd->ihst', query, key_rows) / math.sqrt(head_size)
    causal = jnp.arange(snap_count)[:, None] >= jnp.arange(snap_count)[None, :]
    scores = jnp.where(causal, scores, -1e+30)
    largest = lax.optimization_barrier(jnp.max(scores, axis=-1, keepdims=True))
    expo = jnp.where(causal, jnp.exp(scores - largest), 0.0)
    weights_soft = (expo / lax.optimization_barrier(jnp.sum(expo, axis=-1, keepdims=True))).astype(jnp.bfloat16)
    context = jnp.einsum('ihst,tihd->sihd', weights_soft.astype(jnp.float32), value_rows)
    context = context.astype(jnp.bfloat16).reshape(snap_count, item_count, width)
    residual = mixed + project(context, w_out)
    normed_two = norm_rows(residual, gain_second).astype(jnp.bfloat16)
    hidden = jax.nn.gelu(project(normed_two, w_up)).astype(jnp.bfloat16)
    return (residual + project(hidden, w_down)).astype(jnp.bfloat16)

def reference(features, tile_coord, tile_count, tile_values, w_agg, w_root, time_embed, gain_first, w_qkv, w_out, gain_second, w_up, w_down):
    snap_count, vertex_count, width = features.shape
    row_blocks = VB // TILE
    col_blocks = vertex_count // TILE
    group_count = vertex_count // VB
    slot_index = jnp.arange(group_count * TILES_DEV)
    owner_index = slot_index // TILES_DEV
    local_slot = slot_index % TILES_DEV

    def one_snapshot(packed):
        own_rows, tile_pairs, live_count, tile_block = packed
        blocks = own_rows.reshape(col_blocks, TILE, width)
        chosen = blocks[tile_pairs[:, 1]]
        products = jnp.einsum('tij,tjd->tid', tile_block.astype(jnp.float32), chosen.astype(jnp.float32))
        alive = (local_slot < live_count[owner_index]).astype(jnp.float32)
        products = products * alive[:, None, None]
        target = (owner_index * row_blocks + tile_pairs[:, 0]).astype(jnp.int32)
        summed = jax.ops.segment_sum(products, target, num_segments=col_blocks)
        neighbor_sum = summed.reshape(vertex_count, width).astype(jnp.bfloat16)
        combined = jnp.dot(neighbor_sum, w_agg, preferred_element_type=jnp.float32)
        combined = combined + jnp.dot(own_rows, w_root, preferred_element_type=jnp.float32)
        return jax.nn.gelu(combined).astype(jnp.bfloat16)
    graph_rows = lax.map(one_snapshot, (features, tile_coord, tile_count, tile_values))
    grouped = graph_rows.reshape(snap_count, group_count, VB, width).transpose(1, 0, 2, 3)

    def one_group(rows):
        return temporal(rows, time_embed, gain_first, w_qkv, w_out, gain_second, w_up, w_down)
    mixed_out = lax.map(one_group, grouped)
    return mixed_out.transpose(1, 0, 2, 3).reshape(snap_count, vertex_count, width)
```

```python
import functools
import math

import jax
import jax.numpy as jnp
from jax import lax
from jax.experimental import pallas as pl
from jax.experimental.pallas import tpu as pltpu
from jax.sharding import PartitionSpec as P

HEADS = 8
CORES = 2
MESH = pl.DeviceIdType.MESH
MIB = 1 << 20


def graph_kernel(
    cfg,
    table_ref,
    feat_ref,
    tiles_ref,
    wagg_ref,
    wroot_ref,
    land_ref,
    xbuf,
    tiles_v,
    wagg_v,
    wroot_v,
    acc,
    a_buf,
    stage,
    local_sem,
    send_sem,
    recv_sem,
    a2a_send,
    a2a_recv,
):
    n_vertex, n_tm, chunks, chunk, tile, slots = cfg
    chips = n_vertex // CORES
    local = feat_ref.shape[0]
    row_blocks = local // tile
    col_blocks = n_vertex * row_blocks
    per_chunk = chunk // tile
    item = local // n_tm
    me = lax.axis_index("vertex")
    tm = lax.axis_index("tm")
    z = me // CORES
    core = me % CORES
    sibling = z * CORES + (1 - core)
    has_right = z < chips - 1
    has_left = z > 0

    barrier = pltpu.get_barrier_semaphore()

    def greet(ids):
        pl.semaphore_signal(barrier, inc=1, device_id=ids, device_id_type=MESH)

    greet({"vertex": sibling})

    @pl.when(has_right)
    def _():
        greet({"vertex": me + CORES})

    @pl.when(has_left)
    def _():
        greet({"vertex": me - CORES})

    for i in range(1, n_tm):
        greet({"tm": lax.rem(tm + i, n_tm)})

    own_copy = pltpu.make_async_copy(feat_ref, xbuf.at[me], local_sem.at[0])
    tile_copy = pltpu.make_async_copy(tiles_ref, tiles_v.at[pl.ds(0, slots)], local_sem.at[1])
    agg_copy = pltpu.make_async_copy(wagg_ref, wagg_v, local_sem.at[2])
    root_copy = pltpu.make_async_copy(wroot_ref, wroot_v, local_sem.at[3])
    own_copy.start()
    tile_copy.start()
    agg_copy.start()
    root_copy.start()

    ends = jnp.where(has_right, 1, 0) + jnp.where(has_left, 1, 0)
    pl.semaphore_wait(barrier, n_tm + ends)

    def piece(shard, part, way, target):
        rows = pl.ds(pl.multiple_of(part * chunk, chunk), chunk)
        return pltpu.make_async_remote_copy(
            src_ref=xbuf.at[shard, rows],
            dst_ref=xbuf.at[shard, rows],
            send_sem=send_sem.at[way, shard, part],
            recv_sem=recv_sem.at[shard, part],
            device_id={"vertex": target},
            device_id_type=MESH,
        )

    def spread(shard, part, right, left):
        @pl.when(right)
        def _():
            piece(shard, part, 0, me + CORES).start()

        @pl.when(left)
        def _():
            piece(shard, part, 1, me - CORES).start()

        piece(shard, part, 2, sibling).start()

    def settle(shard, part, right, left):
        @pl.when(right)
        def _():
            piece(shard, part, 0, me + CORES).wait_send()

        @pl.when(left)
        def _():
            piece(shard, part, 1, me - CORES).wait_send()

        piece(shard, part, 2, sibling).wait_send()

    def arrived(shard, part):
        piece(shard, part, 2, sibling).wait_recv()

    def multiply(shard, part):
        first = shard * row_blocks + part * per_chunk
        for r in range(row_blocks):
            for j in range(per_chunk):
                slot = table_ref[r * col_blocks + first + j]
                a_buf[r * tile : (r + 1) * tile, j * tile : (j + 1) * tile] = tiles_v[slot]
        rows = pl.ds(pl.multiple_of(part * chunk, chunk), chunk)
        acc[...] += jnp.dot(a_buf[...], xbuf[shard, rows], preferred_element_type=jnp.float32)

    own_copy.wait()

    def send_own(part, carry):
        spread(me, part, has_right, has_left)
        return carry

    lax.fori_loop(0, chunks, send_own, 0)
    tiles_v[slots] = jnp.zeros(tiles_v.shape[1:], tiles_v.dtype)
    acc[...] = jnp.zeros_like(acc)
    tile_copy.wait()
    agg_copy.wait()
    root_copy.wait()

    def first_step(i, carry):
        part = lax.rem(i, chunks)
        other = i // chunks
        shard = me + other * (sibling - me)

        @pl.when(other == 1)
        def _():
            arrived(shard, part)

        multiply(shard, part)
        return carry

    lax.fori_loop(0, CORES * chunks, first_step, 0)

    def step(i, carry):
        hop = i // chunks + 1
        part = lax.rem(i, chunks)
        low = z - hop
        high = z + hop

        @pl.when(low >= 0)
        def _():
            shard = low * CORES + core
            arrived(shard, part)
            spread(shard, part, has_right, False)

        @pl.when(high < chips)
        def _():
            shard = high * CORES + core
            arrived(shard, part)
            spread(shard, part, False, has_left)

        def use(j, inner):
            side = lax.rem(j, 2)
            other = j // 2
            chip = z - hop + side * 2 * hop
            shard = chip * CORES + core + other * (1 - 2 * core)

            @pl.when(jnp.logical_and(chip >= 0, chip < chips))
            def _():
                @pl.when(other == 1)
                def _():
                    arrived(shard, part)

                multiply(shard, part)

            return inner

        lax.fori_loop(0, 4, use, 0)
        return carry

    lax.fori_loop(0, (chips - 1) * chunks, step, 0)

    def block(i, carry):
        to = lax.rem(tm + i, n_tm)
        rows = pl.ds(pl.multiple_of(to * item, item), item)
        neighbor_sum = acc[rows].astype(jnp.bfloat16)
        combined = jnp.dot(neighbor_sum, wagg_v[...], preferred_element_type=jnp.float32)
        combined += jnp.dot(xbuf[me, rows], wroot_v[...], preferred_element_type=jnp.float32)
        stage[to] = jax.nn.gelu(combined).astype(jnp.bfloat16)

        @pl.when(i < n_tm)
        def _():
            trade(to).start()

        return carry

    def trade(to):
        return pltpu.make_async_remote_copy(
            src_ref=stage.at[to],
            dst_ref=land_ref.at[tm],
            send_sem=a2a_send.at[to],
            recv_sem=a2a_recv.at[tm],
            device_id={"tm": to},
            device_id_type=MESH,
        )

    def landed(source):
        return pltpu.make_async_remote_copy(
            src_ref=stage.at[source],
            dst_ref=land_ref.at[source],
            send_sem=a2a_send.at[source],
            recv_sem=a2a_recv.at[source],
            device_id={"tm": source},
            device_id_type=MESH,
        )

    lax.fori_loop(1, n_tm + 1, block, 0)
    land_ref[tm] = stage[tm]

    def settle_own(part, carry):
        settle(me, part, has_right, has_left)
        return carry

    lax.fori_loop(0, chunks, settle_own, 0)

    def settle_step(i, carry):
        hop = i // chunks + 1
        part = lax.rem(i, chunks)
        low = z - hop
        high = z + hop

        @pl.when(low >= 0)
        def _():
            settle(low * CORES + core, part, has_right, False)

        @pl.when(high < chips)
        def _():
            settle(high * CORES + core, part, False, has_left)

        return carry

    lax.fori_loop(0, (chips - 1) * chunks, settle_step, 0)

    def finish(i, carry):
        partner = lax.rem(tm + i, n_tm)
        trade(partner).wait_send()
        landed(partner).wait_recv()
        return carry

    lax.fori_loop(1, n_tm, finish, 0)


def norm_rows(values, gain):
    scale = lax.rsqrt(jnp.mean(values * values, axis=-1, keepdims=True) + 1e-06)
    return values * scale * gain


def matmul(left, right):
    return jnp.dot(left, right, preferred_element_type=jnp.float32)


def temporal_body(rows_ref, embed_ref, gain1_ref, qkv_ref, wout_ref, gain2_ref, up_ref, down_ref, out_ref):
    snaps, items, width = rows_ref.shape
    head = width // HEADS
    lanes = 128
    size = max(16, min(items, 512 // snaps))
    col_head = lax.broadcasted_iota(jnp.int32, (width, lanes), 0) // head
    gather_heads = (col_head == lax.broadcasted_iota(jnp.int32, (width, lanes), 1)).astype(jnp.bfloat16)
    row_head = lax.broadcasted_iota(jnp.int32, (lanes, width), 1) // head
    widen_heads = (row_head == lax.broadcasted_iota(jnp.int32, (lanes, width), 0)).astype(jnp.bfloat16)

    def body(i, carry):
        at = pl.ds(pl.multiple_of(i * size, size), size)
        embed = embed_ref[...].astype(jnp.float32)
        mixed = jnp.concatenate(
            [rows_ref[t, at].astype(jnp.float32) + embed[t : t + 1] for t in range(snaps)], axis=0
        )
        normed = norm_rows(mixed, gain1_ref[...].astype(jnp.float32)).astype(jnp.bfloat16)
        qkv = matmul(normed, qkv_ref[...]).astype(jnp.bfloat16)
        query = [qkv[t * size : (t + 1) * size, :width].astype(jnp.float32) for t in range(snaps)]
        keys = [qkv[t * size : (t + 1) * size, width : 2 * width].astype(jnp.float32) for t in range(snaps)]
        vals = [qkv[t * size : (t + 1) * size, 2 * width :].astype(jnp.float32) for t in range(snaps)]
        contexts = []
        for t in range(snaps):
            scores = []
            for u in range(t + 1):
                product = query[t] * keys[u]
                upper = product.astype(jnp.bfloat16)
                lower = (product - upper.astype(jnp.float32)).astype(jnp.bfloat16)
                total = matmul(upper, gather_heads) + matmul(lower, gather_heads)
                scores.append(total / math.sqrt(head))
            largest = functools.reduce(jnp.maximum, scores)
            expo = [jnp.exp(s - largest) for s in scores]
            total = functools.reduce(jnp.add, expo)
            context = None
            for u in range(t + 1):
                weight = matmul((expo[u] / total).astype(jnp.bfloat16), widen_heads)
                term = weight * vals[u]
                context = term if context is None else context + term
            contexts.append(context.astype(jnp.bfloat16))
        residual = mixed + matmul(jnp.concatenate(contexts, axis=0), wout_ref[...])
        normed_two = norm_rows(residual, gain2_ref[...].astype(jnp.float32)).astype(jnp.bfloat16)
        hidden = jax.nn.gelu(matmul(normed_two, up_ref[...])).astype(jnp.bfloat16)
        out = (residual + matmul(hidden, down_ref[...])).astype(out_ref.dtype)
        for t in range(snaps):
            out_ref[t, at] = out[t * size : (t + 1) * size]
        return carry

    lax.fori_loop(0, items // size, body, 0)


def per_device(
    features,
    tile_coord,
    tile_count,
    tile_values,
    w_agg,
    w_root,
    time_embed,
    gain_first,
    w_qkv,
    w_out,
    gain_second,
    w_up,
    w_down,
):
    own = features[0]
    pairs = tile_coord[0]
    tiles = tile_values[0]
    local, width = own.shape
    slots, tile = tiles.shape[0], tiles.shape[1]
    n_vertex = lax.axis_size("vertex")
    n_tm = lax.axis_size("tm")
    row_blocks = local // tile
    col_blocks = n_vertex * row_blocks
    chunk = 2 * tile
    chunks = local // chunk
    item = local // n_tm

    slot = jnp.arange(slots, dtype=jnp.int32)
    flat = jnp.where(slot < tile_count[0, 0], pairs[:, 0] * col_blocks + pairs[:, 1], -1)
    spot = jnp.arange(row_blocks * col_blocks, dtype=jnp.int32)
    table = jnp.min(jnp.where(flat[None, :] == spot[:, None], slot[None, :], slots), axis=1)

    anywhere = pl.BlockSpec(memory_space=pl.ANY)
    vmem = pl.BlockSpec(memory_space=pltpu.VMEM)
    landed = pl.pallas_call(
        functools.partial(graph_kernel, (n_vertex, n_tm, chunks, chunk, tile, slots)),
        out_shape=jax.ShapeDtypeStruct((n_tm, item, width), jnp.bfloat16),
        in_specs=[pl.BlockSpec(memory_space=pltpu.SMEM)] + [anywhere] * 4,
        out_specs=vmem,
        scratch_shapes=[
            pltpu.VMEM((n_vertex, local, width), jnp.bfloat16),
            pltpu.VMEM((slots + 1, tile, tile), jnp.bfloat16),
            pltpu.VMEM((width, width), jnp.bfloat16),
            pltpu.VMEM((width, width), jnp.bfloat16),
            pltpu.VMEM((local, width), jnp.float32),
            pltpu.VMEM((local, chunk), jnp.bfloat16),
            pltpu.VMEM((n_tm, item, width), jnp.bfloat16),
            pltpu.SemaphoreType.DMA((4,)),
            pltpu.SemaphoreType.DMA((3, n_vertex, chunks)),
            pltpu.SemaphoreType.DMA((n_vertex, chunks)),
            pltpu.SemaphoreType.DMA((n_tm,)),
            pltpu.SemaphoreType.DMA((n_tm,)),
        ],
        compiler_params=pltpu.CompilerParams(
            collective_id=0, has_side_effects=True, vmem_limit_bytes=44 * MIB
        ),
    )(table, own, tiles, w_agg, w_root)
    return pl.pallas_call(
        temporal_body,
        out_shape=jax.ShapeDtypeStruct((n_tm, item, width), jnp.bfloat16),
        in_specs=[vmem] * 8,
        out_specs=vmem,
        compiler_params=pltpu.CompilerParams(vmem_limit_bytes=44 * MIB),
    )(landed, time_embed, gain_first[None], w_qkv, w_out, gain_second[None], w_up, w_down)


def solution(mesh):
    return jax.shard_map(
        per_device,
        mesh=mesh,
        in_specs=(
            P("tm", "vertex", None),
            P("tm", "vertex", None),
            P("tm", "vertex"),
            P("tm", "vertex", None, None),
            P(),
            P(),
            P(),
            P(),
            P(),
            P(),
            P(),
            P(),
            P(),
        ),
        out_specs=P(None, ("vertex", "tm"), None),
        check_vma=False,
    )
```

```python
import functools
import math

import jax
import jax.numpy as jnp
from jax import lax
from jax.experimental import pallas as pl
from jax.experimental.pallas import tpu as pltpu
from jax.sharding import PartitionSpec as P

HEADS = 8
CORES = 2
MESH = pl.DeviceIdType.MESH
MIB = 1 << 20


def graph_kernel(
    cfg,
    table_ref,
    feat_ref,
    tiles_ref,
    wagg_ref,
    wroot_ref,
    qkv_ref,
    wout_ref,
    up_ref,
    down_ref,
    embed_ref,
    gain1_ref,
    gain2_ref,
    out_ref,
    xbuf,
    tiles_v,
    wagg_v,
    wroot_v,
    qkv_v,
    wout_v,
    up_v,
    down_v,
    acc,
    root,
    a_buf,
    stage,
    land,
    local_sem,
    send_sem,
    recv_sem,
    a2a_send,
    a2a_recv,
):
    n_vertex, n_tm, chunks, chunk, tile, slots, sub = cfg
    chips = n_vertex // CORES
    local = feat_ref.shape[0]
    row_blocks = local // tile
    col_blocks = n_vertex * row_blocks
    per_chunk = chunk // tile
    item = local // n_tm
    me = lax.axis_index("vertex")
    tm = lax.axis_index("tm")
    z = me // CORES
    core = me % CORES
    sibling = z * CORES + (1 - core)
    has_right = z < chips - 1
    has_left = z > 0

    barrier = pltpu.get_barrier_semaphore()

    def greet(ids):
        pl.semaphore_signal(barrier, inc=1, device_id=ids, device_id_type=MESH)

    greet({"vertex": sibling})

    @pl.when(has_right)
    def _():
        greet({"vertex": me + CORES})

    @pl.when(has_left)
    def _():
        greet({"vertex": me - CORES})

    for i in range(1, n_tm):
        greet({"tm": lax.rem(tm + i, n_tm)})

    own_copy = pltpu.make_async_copy(feat_ref, xbuf.at[me], local_sem.at[0])
    tile_copy = pltpu.make_async_copy(tiles_ref, tiles_v.at[pl.ds(0, slots)], local_sem.at[1])
    agg_copy = pltpu.make_async_copy(wagg_ref, wagg_v, local_sem.at[2])
    root_copy = pltpu.make_async_copy(wroot_ref, wroot_v, local_sem.at[3])
    weight_copies = [
        pltpu.make_async_copy(source, target, local_sem.at[4 + i])
        for i, (source, target) in enumerate(
            [(qkv_ref, qkv_v), (wout_ref, wout_v), (up_ref, up_v), (down_ref, down_v)]
        )
    ]
    own_copy.start()

    ends = jnp.where(has_right, 1, 0) + jnp.where(has_left, 1, 0)
    pl.semaphore_wait(barrier, n_tm + ends)

    def piece(shard, part, way, target):
        rows = pl.ds(pl.multiple_of(part * chunk, chunk), chunk)
        return pltpu.make_async_remote_copy(
            src_ref=xbuf.at[shard, rows],
            dst_ref=xbuf.at[shard, rows],
            send_sem=send_sem.at[way, shard, part],
            recv_sem=recv_sem.at[shard, part],
            device_id={"vertex": target},
            device_id_type=MESH,
        )

    def spread(shard, part, right, left):
        @pl.when(right)
        def _():
            piece(shard, part, 0, me + CORES).start()

        @pl.when(left)
        def _():
            piece(shard, part, 1, me - CORES).start()

        piece(shard, part, 2, sibling).start()

    def settle(shard, part, right, left):
        @pl.when(right)
        def _():
            piece(shard, part, 0, me + CORES).wait_send()

        @pl.when(left)
        def _():
            piece(shard, part, 1, me - CORES).wait_send()

        piece(shard, part, 2, sibling).wait_send()

    def arrived(shard, part):
        piece(shard, part, 2, sibling).wait_recv()

    def multiply(shard, part):
        first = shard * row_blocks + part * per_chunk
        for r in range(row_blocks):
            for j in range(per_chunk):
                slot = table_ref[r * col_blocks + first + j]
                a_buf[r * tile : (r + 1) * tile, j * tile : (j + 1) * tile] = tiles_v[slot]
        rows = pl.ds(pl.multiple_of(part * chunk, chunk), chunk)
        acc[...] += jnp.dot(a_buf[...], xbuf[shard, rows], preferred_element_type=jnp.float32)

    own_copy.wait()

    def send_own(part, carry):
        spread(me, part, has_right, has_left)
        return carry

    lax.fori_loop(0, chunks, send_own, 0)
    for copy in [tile_copy, root_copy, agg_copy] + weight_copies:
        copy.start()
    tiles_v[slots] = jnp.zeros(tiles_v.shape[1:], tiles_v.dtype)
    acc[...] = jnp.zeros_like(acc)
    for copy in [tile_copy, root_copy, agg_copy] + weight_copies:
        copy.wait()
    root[...] = jnp.dot(xbuf[me], wroot_v[...], preferred_element_type=jnp.float32)

    def first_step(i, carry):
        part = lax.rem(i, chunks)
        other = i // chunks
        shard = me + other * (sibling - me)

        @pl.when(other == 1)
        def _():
            arrived(shard, part)

        multiply(shard, part)
        return carry

    lax.fori_loop(0, CORES * chunks, first_step, 0)

    def step(i, carry):
        hop = i // chunks + 1
        part = lax.rem(i, chunks)
        low = z - hop
        high = z + hop

        @pl.when(low >= 0)
        def _():
            shard = low * CORES + core
            arrived(shard, part)
            spread(shard, part, has_right, False)

        @pl.when(high < chips)
        def _():
            shard = high * CORES + core
            arrived(shard, part)
            spread(shard, part, False, has_left)

        def use(j, inner):
            side = lax.rem(j, 2)
            other = j // 2
            chip = z - hop + side * 2 * hop
            shard = chip * CORES + core + other * (1 - 2 * core)

            @pl.when(jnp.logical_and(chip >= 0, chip < chips))
            def _():
                @pl.when(other == 1)
                def _():
                    arrived(shard, part)

                multiply(shard, part)

            return inner

        lax.fori_loop(0, 4, use, 0)
        return carry

    lax.fori_loop(0, (chips - 1) * chunks, step, 0)

    def trade(to, part):
        rows = pl.ds(pl.multiple_of(part * sub, sub), sub)
        return pltpu.make_async_remote_copy(
            src_ref=stage.at[to, rows],
            dst_ref=land.at[tm, rows],
            send_sem=a2a_send.at[to, part],
            recv_sem=a2a_recv.at[tm, part],
            device_id={"tm": to},
            device_id_type=MESH,
        )

    def landed(source, part):
        rows = pl.ds(pl.multiple_of(part * sub, sub), sub)
        return pltpu.make_async_remote_copy(
            src_ref=stage.at[source, rows],
            dst_ref=land.at[source, rows],
            send_sem=a2a_send.at[source, part],
            recv_sem=a2a_recv.at[source, part],
            device_id={"tm": source},
            device_id_type=MESH,
        )

    def block(part, carry):
        def rows_of(to):
            return pl.ds(pl.multiple_of(to * item + part * sub, sub), sub)

        here = pl.ds(pl.multiple_of(part * sub, sub), sub)
        summed = jnp.concatenate([acc[rows_of(to)] for to in range(n_tm)], axis=0)
        based = jnp.concatenate([root[rows_of(to)] for to in range(n_tm)], axis=0)
        combined = based + matmul(summed.astype(jnp.bfloat16), wagg_v[...])
        graph_rows = jax.nn.gelu(combined).astype(jnp.bfloat16)
        for to in range(n_tm):
            stage[to, here] = graph_rows[to * sub : (to + 1) * sub]

        def send(i, inner):
            trade(lax.rem(tm + i, n_tm), part).start()
            return inner

        lax.fori_loop(1, n_tm, send, 0)
        land[tm, here] = stage[tm, here]
        return carry

    lax.fori_loop(0, item // sub, block, 0)

    def await_rows(part):
        def one(i, inner):
            landed(lax.rem(tm + i, n_tm), part).wait_recv()
            return inner

        lax.fori_loop(1, n_tm, one, 0)

    temporal_body(
        await_rows, sub, land, embed_ref, gain1_ref, qkv_v, wout_v, gain2_ref, up_v, down_v, out_ref
    )

    def settle_own(part, carry):
        settle(me, part, has_right, has_left)
        return carry

    lax.fori_loop(0, chunks, settle_own, 0)

    def settle_step(i, carry):
        hop = i // chunks + 1
        part = lax.rem(i, chunks)
        low = z - hop
        high = z + hop

        @pl.when(low >= 0)
        def _():
            settle(low * CORES + core, part, has_right, False)

        @pl.when(high < chips)
        def _():
            settle(high * CORES + core, part, False, has_left)

        return carry

    lax.fori_loop(0, (chips - 1) * chunks, settle_step, 0)

    def finish(i, carry):
        trade(lax.rem(tm + 1 + i // (item // sub), n_tm), lax.rem(i, item // sub)).wait_send()
        return carry

    lax.fori_loop(0, (n_tm - 1) * (item // sub), finish, 0)


def norm_rows(values, gain):
    scale = lax.rsqrt(jnp.mean(values * values, axis=-1, keepdims=True) + 1e-06)
    return values * scale * gain


def matmul(left, right):
    return jnp.dot(left, right, preferred_element_type=jnp.float32)


def temporal_body(
    await_rows, size, rows_ref, embed_ref, gain1_ref, qkv_ref, wout_ref, gain2_ref, up_ref, down_ref, out_ref
):
    snaps, items, width = rows_ref.shape
    head = width // HEADS
    lanes = 128
    col_head = lax.broadcasted_iota(jnp.int32, (width, lanes), 0) // head
    gather_heads = (col_head == lax.broadcasted_iota(jnp.int32, (width, lanes), 1)).astype(jnp.bfloat16)
    row_head = lax.broadcasted_iota(jnp.int32, (lanes, width), 1) // head
    widen_heads = (row_head == lax.broadcasted_iota(jnp.int32, (lanes, width), 0)).astype(jnp.bfloat16)

    def body(i, carry):
        await_rows(i)
        at = pl.ds(pl.multiple_of(i * size, size), size)
        embed = embed_ref[...].astype(jnp.float32)
        mixed = jnp.concatenate(
            [rows_ref[t, at].astype(jnp.float32) + embed[t : t + 1] for t in range(snaps)], axis=0
        )
        normed = norm_rows(mixed, gain1_ref[...].astype(jnp.float32)[None]).astype(jnp.bfloat16)
        qkv = matmul(normed, qkv_ref[...]).astype(jnp.bfloat16)
        query = [qkv[t * size : (t + 1) * size, :width].astype(jnp.float32) for t in range(snaps)]
        keys = [qkv[t * size : (t + 1) * size, width : 2 * width].astype(jnp.float32) for t in range(snaps)]
        vals = [qkv[t * size : (t + 1) * size, 2 * width :].astype(jnp.float32) for t in range(snaps)]
        contexts = []
        for t in range(snaps):
            scores = []
            for u in range(t + 1):
                product = query[t] * keys[u]
                upper = product.astype(jnp.bfloat16)
                lower = (product - upper.astype(jnp.float32)).astype(jnp.bfloat16)
                total = matmul(upper, gather_heads) + matmul(lower, gather_heads)
                scores.append(total / math.sqrt(head))
            largest = functools.reduce(jnp.maximum, scores)
            expo = [jnp.exp(s - largest) for s in scores]
            total = functools.reduce(jnp.add, expo)
            context = None
            for u in range(t + 1):
                weight = matmul((expo[u] / total).astype(jnp.bfloat16), widen_heads)
                term = weight * vals[u]
                context = term if context is None else context + term
            contexts.append(context.astype(jnp.bfloat16))
        residual = mixed + matmul(jnp.concatenate(contexts, axis=0), wout_ref[...])
        normed_two = norm_rows(residual, gain2_ref[...].astype(jnp.float32)[None]).astype(jnp.bfloat16)
        hidden = jax.nn.gelu(matmul(normed_two, up_ref[...])).astype(jnp.bfloat16)
        out = (residual + matmul(hidden, down_ref[...])).astype(out_ref.dtype)
        for t in range(snaps):
            out_ref[t, at] = out[t * size : (t + 1) * size]
        return carry

    lax.fori_loop(0, items // size, body, 0)


def per_device(
    features,
    tile_coord,
    tile_count,
    tile_values,
    w_agg,
    w_root,
    time_embed,
    gain_first,
    w_qkv,
    w_out,
    gain_second,
    w_up,
    w_down,
):
    own = features[0]
    pairs = tile_coord[0]
    tiles = tile_values[0]
    local, width = own.shape
    slots, tile = tiles.shape[0], tiles.shape[1]
    n_vertex = lax.axis_size("vertex")
    n_tm = lax.axis_size("tm")
    row_blocks = local // tile
    col_blocks = n_vertex * row_blocks
    chunk = 2 * tile
    chunks = local // chunk
    item = local // n_tm
    sub = max(16, min(item, 256 // n_tm))

    slot = jnp.arange(slots, dtype=jnp.int32)
    flat = jnp.where(slot < tile_count[0, 0], pairs[:, 0] * col_blocks + pairs[:, 1], -1)
    spot = jnp.arange(row_blocks * col_blocks, dtype=jnp.int32)
    table = jnp.min(jnp.where(flat[None, :] == spot[:, None], slot[None, :], slots), axis=1)

    anywhere = pl.BlockSpec(memory_space=pl.ANY)
    vmem = pl.BlockSpec(memory_space=pltpu.VMEM)
    return pl.pallas_call(
        functools.partial(graph_kernel, (n_vertex, n_tm, chunks, chunk, tile, slots, sub)),
        out_shape=jax.ShapeDtypeStruct((n_tm, item, width), jnp.bfloat16),
        in_specs=[pl.BlockSpec(memory_space=pltpu.SMEM)] + [anywhere] * 8 + [vmem] * 3,
        out_specs=vmem,
        scratch_shapes=[
            pltpu.VMEM((n_vertex, local, width), jnp.bfloat16),
            pltpu.VMEM((slots + 1, tile, tile), jnp.bfloat16),
            pltpu.VMEM(w_agg.shape, jnp.bfloat16),
            pltpu.VMEM(w_root.shape, jnp.bfloat16),
            pltpu.VMEM(w_qkv.shape, jnp.bfloat16),
            pltpu.VMEM(w_out.shape, jnp.bfloat16),
            pltpu.VMEM(w_up.shape, jnp.bfloat16),
            pltpu.VMEM(w_down.shape, jnp.bfloat16),
            pltpu.VMEM((local, width), jnp.float32),
            pltpu.VMEM((local, width), jnp.float32),
            pltpu.VMEM((local, chunk), jnp.bfloat16),
            pltpu.VMEM((n_tm, item, width), jnp.bfloat16),
            pltpu.VMEM((n_tm, item, width), jnp.bfloat16),
            pltpu.SemaphoreType.DMA((8,)),
            pltpu.SemaphoreType.DMA((3, n_vertex, chunks)),
            pltpu.SemaphoreType.DMA((n_vertex, chunks)),
            pltpu.SemaphoreType.DMA((n_tm, item // sub)),
            pltpu.SemaphoreType.DMA((n_tm, item // sub)),
        ],
        compiler_params=pltpu.CompilerParams(
            collective_id=0, has_side_effects=True, vmem_limit_bytes=56 * MIB
        ),
    )(table, own, tiles, w_agg, w_root, w_qkv, w_out, w_up, w_down, time_embed, gain_first, gain_second)


def solution(mesh):
    return jax.shard_map(
        per_device,
        mesh=mesh,
        in_specs=(
            P("tm", "vertex", None),
            P("tm", "vertex", None),
            P("tm", "vertex"),
            P("tm", "vertex", None, None),
            P(),
            P(),
            P(),
            P(),
            P(),
            P(),
            P(),
            P(),
            P(),
        ),
        out_specs=P(None, ("vertex", "tm"), None),
        check_vma=False,
    )
```

```python
import functools
import math

import jax
import jax.numpy as jnp
from jax import lax
from jax.experimental import pallas as pl
from jax.experimental.pallas import tpu as pltpu
from jax.sharding import PartitionSpec as P

HEADS = 8
CORES = 2
MESH = pl.DeviceIdType.MESH
MIB = 1 << 20
LANES = 128


def fill_table(live, pairs_ref, table_ref, slots, col_blocks):
    lane = lax.broadcasted_iota(jnp.int32, (1, slots), 1)
    flat = pairs_ref[0:1] * col_blocks + pairs_ref[1:2]
    flat = jnp.where(lane < live, flat, -1)
    wide = jnp.broadcast_to(flat, (LANES, slots)).T
    slot = lax.broadcasted_iota(jnp.int32, (slots, LANES), 0)
    column = lax.broadcasted_iota(jnp.int32, (slots, LANES), 1)
    for row in range(table_ref.shape[0]):
        hit = jnp.where(wide == column + row * LANES, slot, slots)
        table_ref[row : row + 1] = jnp.min(hit, axis=0, keepdims=True)


def graph_kernel(
    cfg,
    count_ref,
    pairs_ref,
    feat_ref,
    tiles_ref,
    wagg_ref,
    wroot_ref,
    qkv_ref,
    wout_ref,
    up_ref,
    down_ref,
    embed_ref,
    gain1_ref,
    gain2_ref,
    out_ref,
    xbuf,
    tiles_v,
    wagg_v,
    wroot_v,
    qkv_v,
    wout_v,
    up_v,
    down_v,
    acc,
    root,
    a_buf,
    stage,
    land,
    table_v,
    table_s,
    local_sem,
    send_sem,
    recv_sem,
    a2a_send,
    a2a_recv,
):
    n_vertex, n_tm, chunks, chunk, tile, slots, sub = cfg
    chips = n_vertex // CORES
    local = feat_ref.shape[0]
    row_blocks = local // tile
    col_blocks = n_vertex * row_blocks
    per_chunk = chunk // tile
    item = local // n_tm
    me = lax.axis_index("vertex")
    tm = lax.axis_index("tm")
    z = me // CORES
    core = me % CORES
    sibling = z * CORES + (1 - core)
    has_right = z < chips - 1
    has_left = z > 0

    barrier = pltpu.get_barrier_semaphore()

    def greet(ids):
        pl.semaphore_signal(barrier, inc=1, device_id=ids, device_id_type=MESH)

    greet({"vertex": sibling})

    @pl.when(has_right)
    def _():
        greet({"vertex": me + CORES})

    @pl.when(has_left)
    def _():
        greet({"vertex": me - CORES})

    for i in range(1, n_tm):
        greet({"tm": lax.rem(tm + i, n_tm)})

    own_copy = pltpu.make_async_copy(feat_ref, xbuf.at[me], local_sem.at[0])
    tile_copy = pltpu.make_async_copy(tiles_ref, tiles_v.at[pl.ds(0, slots)], local_sem.at[1])
    agg_copy = pltpu.make_async_copy(wagg_ref, wagg_v, local_sem.at[2])
    root_copy = pltpu.make_async_copy(wroot_ref, wroot_v, local_sem.at[3])
    weight_copies = [
        pltpu.make_async_copy(source, target, local_sem.at[4 + i])
        for i, (source, target) in enumerate(
            [(qkv_ref, qkv_v), (wout_ref, wout_v), (up_ref, up_v), (down_ref, down_v)]
        )
    ]
    own_copy.start()

    ends = jnp.where(has_right, 1, 0) + jnp.where(has_left, 1, 0)
    pl.semaphore_wait(barrier, n_tm + ends)

    def piece(shard, part, way, target):
        rows = pl.ds(pl.multiple_of(part * chunk, chunk), chunk)
        return pltpu.make_async_remote_copy(
            src_ref=xbuf.at[shard, rows],
            dst_ref=xbuf.at[shard, rows],
            send_sem=send_sem.at[way, shard, part],
            recv_sem=recv_sem.at[shard, part],
            device_id={"vertex": target},
            device_id_type=MESH,
        )

    def spread(shard, part, right, left):
        @pl.when(right)
        def _():
            piece(shard, part, 0, me + CORES).start()

        @pl.when(left)
        def _():
            piece(shard, part, 1, me - CORES).start()

        piece(shard, part, 2, sibling).start()

    def settle(shard, part, right, left):
        @pl.when(right)
        def _():
            piece(shard, part, 0, me + CORES).wait_send()

        @pl.when(left)
        def _():
            piece(shard, part, 1, me - CORES).wait_send()

        piece(shard, part, 2, sibling).wait_send()

    def arrived(shard, part):
        piece(shard, part, 2, sibling).wait_recv()

    def multiply(shard, part):
        first = shard * row_blocks + part * per_chunk
        for r in range(row_blocks):
            for j in range(per_chunk):
                spot = r * col_blocks + first + j
                slot = table_s[spot // LANES, lax.rem(spot, LANES)]
                a_buf[r * tile : (r + 1) * tile, j * tile : (j + 1) * tile] = tiles_v[slot]
        rows = pl.ds(pl.multiple_of(part * chunk, chunk), chunk)
        acc[...] += jnp.dot(a_buf[...], xbuf[shard, rows], preferred_element_type=jnp.float32)

    own_copy.wait()

    def send_own(part, carry):
        spread(me, part, has_right, has_left)
        return carry

    lax.fori_loop(0, chunks, send_own, 0)
    for copy in [tile_copy, root_copy, agg_copy] + weight_copies:
        copy.start()
    fill_table(count_ref[0, 0], pairs_ref, table_v, slots, col_blocks)
    table_copy = pltpu.make_async_copy(table_v, table_s, local_sem.at[8])
    table_copy.start()
    tiles_v[slots] = jnp.zeros(tiles_v.shape[1:], tiles_v.dtype)
    acc[...] = jnp.zeros_like(acc)
    for copy in [tile_copy, root_copy, agg_copy] + weight_copies:
        copy.wait()
    table_copy.wait()
    root[...] = jnp.dot(xbuf[me], wroot_v[...], preferred_element_type=jnp.float32)

    def first_step(i, carry):
        part = lax.rem(i, chunks)
        other = i // chunks
        shard = me + other * (sibling - me)

        @pl.when(other == 1)
        def _():
            arrived(shard, part)

        multiply(shard, part)
        return carry

    lax.fori_loop(0, CORES * chunks, first_step, 0)

    def step(i, carry):
        hop = i // chunks + 1
        part = lax.rem(i, chunks)
        low = z - hop
        high = z + hop

        @pl.when(low >= 0)
        def _():
            shard = low * CORES + core
            arrived(shard, part)
            spread(shard, part, has_right, False)

        @pl.when(high < chips)
        def _():
            shard = high * CORES + core
            arrived(shard, part)
            spread(shard, part, False, has_left)

        def use(j, inner):
            side = lax.rem(j, 2)
            other = j // 2
            chip = z - hop + side * 2 * hop
            shard = chip * CORES + core + other * (1 - 2 * core)

            @pl.when(jnp.logical_and(chip >= 0, chip < chips))
            def _():
                @pl.when(other == 1)
                def _():
                    arrived(shard, part)

                multiply(shard, part)

            return inner

        lax.fori_loop(0, 4, use, 0)
        return carry

    lax.fori_loop(0, (chips - 1) * chunks, step, 0)

    def trade(to, part):
        rows = pl.ds(pl.multiple_of(part * sub, sub), sub)
        return pltpu.make_async_remote_copy(
            src_ref=stage.at[to, rows],
            dst_ref=land.at[tm, rows],
            send_sem=a2a_send.at[to, part],
            recv_sem=a2a_recv.at[tm, part],
            device_id={"tm": to},
            device_id_type=MESH,
        )

    def landed(source, part):
        rows = pl.ds(pl.multiple_of(part * sub, sub), sub)
        return pltpu.make_async_remote_copy(
            src_ref=stage.at[source, rows],
            dst_ref=land.at[source, rows],
            send_sem=a2a_send.at[source, part],
            recv_sem=a2a_recv.at[source, part],
            device_id={"tm": source},
            device_id_type=MESH,
        )

    def block(part, carry):
        def rows_of(to):
            return pl.ds(pl.multiple_of(to * item + part * sub, sub), sub)

        here = pl.ds(pl.multiple_of(part * sub, sub), sub)
        summed = jnp.concatenate([acc[rows_of(to)] for to in range(n_tm)], axis=0)
        based = jnp.concatenate([root[rows_of(to)] for to in range(n_tm)], axis=0)
        combined = based + matmul(summed.astype(jnp.bfloat16), wagg_v[...])
        graph_rows = jax.nn.gelu(combined).astype(jnp.bfloat16)
        for to in range(n_tm):
            stage[to, here] = graph_rows[to * sub : (to + 1) * sub]

        def send(i, inner):
            trade(lax.rem(tm + i, n_tm), part).start()
            return inner

        lax.fori_loop(1, n_tm, send, 0)
        land[tm, here] = stage[tm, here]
        return carry

    lax.fori_loop(0, item // sub, block, 0)

    def await_rows(part):
        def one(i, inner):
            landed(lax.rem(tm + i, n_tm), part).wait_recv()
            return inner

        lax.fori_loop(1, n_tm, one, 0)

    temporal_body(
        await_rows, sub, land, embed_ref, gain1_ref, qkv_v, wout_v, gain2_ref, up_v, down_v, out_ref
    )

    def settle_own(part, carry):
        settle(me, part, has_right, has_left)
        return carry

    lax.fori_loop(0, chunks, settle_own, 0)

    def settle_step(i, carry):
        hop = i // chunks + 1
        part = lax.rem(i, chunks)
        low = z - hop
        high = z + hop

        @pl.when(low >= 0)
        def _():
            settle(low * CORES + core, part, has_right, False)

        @pl.when(high < chips)
        def _():
            settle(high * CORES + core, part, False, has_left)

        return carry

    lax.fori_loop(0, (chips - 1) * chunks, settle_step, 0)

    def finish(i, carry):
        trade(lax.rem(tm + 1 + i // (item // sub), n_tm), lax.rem(i, item // sub)).wait_send()
        return carry

    lax.fori_loop(0, (n_tm - 1) * (item // sub), finish, 0)


def norm_rows(values, gain):
    scale = lax.rsqrt(jnp.mean(values * values, axis=-1, keepdims=True) + 1e-06)
    return values * scale * gain


def matmul(left, right):
    return jnp.dot(left, right, preferred_element_type=jnp.float32)


def temporal_body(
    await_rows, size, rows_ref, embed_ref, gain1_ref, qkv_ref, wout_ref, gain2_ref, up_ref, down_ref, out_ref
):
    snaps, items, width = rows_ref.shape
    head = width // HEADS
    lanes = 128
    col_head = lax.broadcasted_iota(jnp.int32, (width, lanes), 0) // head
    gather_heads = (col_head == lax.broadcasted_iota(jnp.int32, (width, lanes), 1)).astype(jnp.bfloat16)
    row_head = lax.broadcasted_iota(jnp.int32, (lanes, width), 1) // head
    widen_heads = (row_head == lax.broadcasted_iota(jnp.int32, (lanes, width), 0)).astype(jnp.bfloat16)

    def body(i, carry):
        await_rows(i)
        at = pl.ds(pl.multiple_of(i * size, size), size)
        embed = embed_ref[...].astype(jnp.float32)
        mixed = jnp.concatenate(
            [rows_ref[t, at].astype(jnp.float32) + embed[t : t + 1] for t in range(snaps)], axis=0
        )
        normed = norm_rows(mixed, gain1_ref[...].astype(jnp.float32)[None]).astype(jnp.bfloat16)
        qkv = matmul(normed, qkv_ref[...]).astype(jnp.bfloat16)
        query = [qkv[t * size : (t + 1) * size, :width].astype(jnp.float32) for t in range(snaps)]
        keys = [qkv[t * size : (t + 1) * size, width : 2 * width].astype(jnp.float32) for t in range(snaps)]
        vals = [qkv[t * size : (t + 1) * size, 2 * width :].astype(jnp.float32) for t in range(snaps)]
        uppers, lowers = [], []
        for t in range(snaps):
            for u in range(t + 1):
                product = query[t] * keys[u]
                upper = product.astype(jnp.bfloat16)
                uppers.append(upper)
                lowers.append((product - upper.astype(jnp.float32)).astype(jnp.bfloat16))
        totals = matmul(jnp.concatenate(uppers + lowers, axis=0), gather_heads)
        count = len(uppers) * size
        all_scores = (totals[:count] + totals[count:]) / math.sqrt(head)
        weights = []
        for t in range(snaps):
            first = t * (t + 1) // 2
            scores = [all_scores[(first + u) * size : (first + u + 1) * size] for u in range(t + 1)]
            largest = functools.reduce(jnp.maximum, scores)
            expo = [jnp.exp(score - largest) for score in scores]
            total = functools.reduce(jnp.add, expo)
            weights += [(each / total).astype(jnp.bfloat16) for each in expo]
        wide = matmul(jnp.concatenate(weights, axis=0), widen_heads)
        contexts = []
        for t in range(snaps):
            first = t * (t + 1) // 2
            terms = [wide[(first + u) * size : (first + u + 1) * size] * vals[u] for u in range(t + 1)]
            contexts.append(functools.reduce(jnp.add, terms).astype(jnp.bfloat16))
        residual = mixed + matmul(jnp.concatenate(contexts, axis=0), wout_ref[...])
        normed_two = norm_rows(residual, gain2_ref[...].astype(jnp.float32)[None]).astype(jnp.bfloat16)
        hidden = jax.nn.gelu(matmul(normed_two, up_ref[...])).astype(jnp.bfloat16)
        out = (residual + matmul(hidden, down_ref[...])).astype(out_ref.dtype)
        for t in range(snaps):
            out_ref[t, at] = out[t * size : (t + 1) * size]
        return carry

    lax.fori_loop(0, items // size, body, 0)


def per_device(
    features,
    tile_coord,
    tile_count,
    tile_values,
    w_agg,
    w_root,
    time_embed,
    gain_first,
    w_qkv,
    w_out,
    gain_second,
    w_up,
    w_down,
):
    own = features[0]
    pairs = tile_coord[0]
    tiles = tile_values[0]
    local, width = own.shape
    slots, tile = tiles.shape[0], tiles.shape[1]
    n_vertex = lax.axis_size("vertex")
    n_tm = lax.axis_size("tm")
    row_blocks = local // tile
    col_blocks = n_vertex * row_blocks
    chunk = 2 * tile
    chunks = local // chunk
    item = local // n_tm
    sub = max(16, min(item, 256 // n_tm))

    anywhere = pl.BlockSpec(memory_space=pl.ANY)
    vmem = pl.BlockSpec(memory_space=pltpu.VMEM)
    return pl.pallas_call(
        functools.partial(graph_kernel, (n_vertex, n_tm, chunks, chunk, tile, slots, sub)),
        out_shape=jax.ShapeDtypeStruct((n_tm, item, width), jnp.bfloat16),
        in_specs=[pl.BlockSpec(memory_space=pltpu.SMEM), vmem] + [anywhere] * 8 + [vmem] * 3,
        out_specs=vmem,
        scratch_shapes=[
            pltpu.VMEM((n_vertex, local, width), jnp.bfloat16),
            pltpu.VMEM((slots + 1, tile, tile), jnp.bfloat16),
            pltpu.VMEM(w_agg.shape, jnp.bfloat16),
            pltpu.VMEM(w_root.shape, jnp.bfloat16),
            pltpu.VMEM(w_qkv.shape, jnp.bfloat16),
            pltpu.VMEM(w_out.shape, jnp.bfloat16),
            pltpu.VMEM(w_up.shape, jnp.bfloat16),
            pltpu.VMEM(w_down.shape, jnp.bfloat16),
            pltpu.VMEM((local, width), jnp.float32),
            pltpu.VMEM((local, width), jnp.float32),
            pltpu.VMEM((local, chunk), jnp.bfloat16),
            pltpu.VMEM((n_tm, item, width), jnp.bfloat16),
            pltpu.VMEM((n_tm, item, width), jnp.bfloat16),
            pltpu.VMEM((row_blocks * col_blocks // LANES, LANES), jnp.int32),
            pltpu.SMEM((row_blocks * col_blocks // LANES, LANES), jnp.int32),
            pltpu.SemaphoreType.DMA((9,)),
            pltpu.SemaphoreType.DMA((3, n_vertex, chunks)),
            pltpu.SemaphoreType.DMA((n_vertex, chunks)),
            pltpu.SemaphoreType.DMA((n_tm, item // sub)),
            pltpu.SemaphoreType.DMA((n_tm, item // sub)),
        ],
        compiler_params=pltpu.CompilerParams(
            collective_id=0, has_side_effects=True, vmem_limit_bytes=56 * MIB
        ),
    )(tile_count, pairs.T, own, tiles, w_agg, w_root, w_qkv, w_out, w_up, w_down, time_embed, gain_first, gain_second)


def solution(mesh):
    return jax.shard_map(
        per_device,
        mesh=mesh,
        in_specs=(
            P("tm", "vertex", None),
            P("tm", "vertex", None),
            P("tm", "vertex"),
            P("tm", "vertex", None, None),
            P(),
            P(),
            P(),
            P(),
            P(),
            P(),
            P(),
            P(),
            P(),
        ),
        out_specs=P(None, ("vertex", "tm"), None),
        check_vma=False,
    )
```

```python
import functools
import math

import jax
import jax.numpy as jnp
from jax import lax
from jax.experimental import pallas as pl
from jax.experimental.pallas import tpu as pltpu
from jax.sharding import PartitionSpec as P

HEADS = 8
CORES = 2
MESH = pl.DeviceIdType.MESH
MIB = 1 << 20
LANES = 128


def fill_table(live, pairs_ref, table_ref, slots, col_blocks):
    lane = lax.broadcasted_iota(jnp.int32, (1, slots), 1)
    flat = pairs_ref[0:1] * col_blocks + pairs_ref[1:2]
    flat = jnp.where(lane < live, flat, -1)
    wide = jnp.broadcast_to(flat, (LANES, slots)).T
    slot = lax.broadcasted_iota(jnp.int32, (slots, LANES), 0)
    column = lax.broadcasted_iota(jnp.int32, (slots, LANES), 1)
    for row in range(table_ref.shape[0]):
        hit = jnp.where(wide == column + row * LANES, slot, slots)
        table_ref[row : row + 1] = jnp.min(hit, axis=0, keepdims=True)


def graph_kernel(
    cfg,
    count_ref,
    pairs_ref,
    feat_ref,
    tiles_ref,
    wagg_ref,
    wroot_ref,
    qkv_ref,
    wout_ref,
    up_ref,
    down_ref,
    embed_ref,
    gain1_ref,
    gain2_ref,
    out_ref,
    xbuf,
    tiles_v,
    wagg_v,
    wroot_v,
    qkv_v,
    wout_v,
    up_v,
    down_v,
    acc,
    root,
    a_buf,
    stage,
    land,
    out_v,
    out_sem,
    table_v,
    table_s,
    local_sem,
    send_sem,
    recv_sem,
    a2a_send,
    a2a_recv,
):
    n_vertex, n_tm, chunks, chunk, tile, slots, sub = cfg
    chips = n_vertex // CORES
    local = feat_ref.shape[0]
    row_blocks = local // tile
    col_blocks = n_vertex * row_blocks
    per_chunk = chunk // tile
    item = local // n_tm
    me = lax.axis_index("vertex")
    tm = lax.axis_index("tm")
    z = me // CORES
    core = me % CORES
    sibling = z * CORES + (1 - core)
    has_right = z < chips - 1
    has_left = z > 0

    barrier = pltpu.get_barrier_semaphore()

    def greet(ids):
        pl.semaphore_signal(barrier, inc=1, device_id=ids, device_id_type=MESH)

    greet({"vertex": sibling})

    @pl.when(has_right)
    def _():
        greet({"vertex": me + CORES})

    @pl.when(has_left)
    def _():
        greet({"vertex": me - CORES})

    for i in range(1, n_tm):
        greet({"tm": lax.rem(tm + i, n_tm)})

    own_copy = pltpu.make_async_copy(feat_ref, xbuf.at[me], local_sem.at[0])
    tile_copy = pltpu.make_async_copy(tiles_ref, tiles_v.at[pl.ds(0, slots)], local_sem.at[1])
    agg_copy = pltpu.make_async_copy(wagg_ref, wagg_v, local_sem.at[2])
    root_copy = pltpu.make_async_copy(wroot_ref, wroot_v, local_sem.at[3])
    weight_copies = [
        pltpu.make_async_copy(source, target, local_sem.at[4 + i])
        for i, (source, target) in enumerate(
            [(qkv_ref, qkv_v), (wout_ref, wout_v), (up_ref, up_v), (down_ref, down_v)]
        )
    ]
    own_copy.start()

    ends = jnp.where(has_right, 1, 0) + jnp.where(has_left, 1, 0)
    pl.semaphore_wait(barrier, n_tm + ends)

    def piece(shard, part, way, target):
        rows = pl.ds(pl.multiple_of(part * chunk, chunk), chunk)
        return pltpu.make_async_remote_copy(
            src_ref=xbuf.at[shard, rows],
            dst_ref=xbuf.at[shard, rows],
            send_sem=send_sem.at[way, shard, part],
            recv_sem=recv_sem.at[shard, part],
            device_id={"vertex": target},
            device_id_type=MESH,
        )

    def spread(shard, part, right, left):
        @pl.when(right)
        def _():
            piece(shard, part, 0, me + CORES).start()

        @pl.when(left)
        def _():
            piece(shard, part, 1, me - CORES).start()

        piece(shard, part, 2, sibling).start()

    def settle(shard, part, right, left):
        @pl.when(right)
        def _():
            piece(shard, part, 0, me + CORES).wait_send()

        @pl.when(left)
        def _():
            piece(shard, part, 1, me - CORES).wait_send()

        piece(shard, part, 2, sibling).wait_send()

    def arrived(shard, part):
        piece(shard, part, 2, sibling).wait_recv()

    def multiply(shard, part):
        first = shard * row_blocks + part * per_chunk
        for r in range(row_blocks):
            for j in range(per_chunk):
                spot = r * col_blocks + first + j
                slot = table_s[spot // LANES, lax.rem(spot, LANES)]
                a_buf[r * tile : (r + 1) * tile, j * tile : (j + 1) * tile] = tiles_v[slot]
        rows = pl.ds(pl.multiple_of(part * chunk, chunk), chunk)
        acc[...] += jnp.dot(a_buf[...], xbuf[shard, rows], preferred_element_type=jnp.float32)

    own_copy.wait()

    def send_own(part, carry):
        spread(me, part, has_right, has_left)
        return carry

    lax.fori_loop(0, chunks, send_own, 0)
    for copy in [tile_copy, root_copy, agg_copy] + weight_copies:
        copy.start()
    fill_table(count_ref[0, 0], pairs_ref, table_v, slots, col_blocks)
    table_copy = pltpu.make_async_copy(table_v, table_s, local_sem.at[8])
    table_copy.start()
    tiles_v[slots] = jnp.zeros(tiles_v.shape[1:], tiles_v.dtype)
    acc[...] = jnp.zeros_like(acc)
    for copy in [tile_copy, root_copy, agg_copy] + weight_copies:
        copy.wait()
    table_copy.wait()
    root[...] = jnp.dot(xbuf[me], wroot_v[...], preferred_element_type=jnp.float32)

    def first_step(i, carry):
        part = lax.rem(i, chunks)
        other = i // chunks
        shard = me + other * (sibling - me)

        @pl.when(other == 1)
        def _():
            arrived(shard, part)

        multiply(shard, part)
        return carry

    lax.fori_loop(0, CORES * chunks, first_step, 0)

    def step(i, carry):
        hop = i // chunks + 1
        part = lax.rem(i, chunks)
        low = z - hop
        high = z + hop

        @pl.when(low >= 0)
        def _():
            shard = low * CORES + core
            arrived(shard, part)
            spread(shard, part, has_right, False)

        @pl.when(high < chips)
        def _():
            shard = high * CORES + core
            arrived(shard, part)
            spread(shard, part, False, has_left)

        def use(j, inner):
            side = lax.rem(j, 2)
            other = j // 2
            chip = z - hop + side * 2 * hop
            shard = chip * CORES + core + other * (1 - 2 * core)

            @pl.when(jnp.logical_and(chip >= 0, chip < chips))
            def _():
                @pl.when(other == 1)
                def _():
                    arrived(shard, part)

                multiply(shard, part)

            return inner

        lax.fori_loop(0, 4, use, 0)
        return carry

    lax.fori_loop(0, (chips - 1) * chunks, step, 0)

    def trade(to, part):
        rows = pl.ds(pl.multiple_of(part * sub, sub), sub)
        return pltpu.make_async_remote_copy(
            src_ref=stage.at[to, rows],
            dst_ref=land.at[tm, rows],
            send_sem=a2a_send.at[to, part],
            recv_sem=a2a_recv.at[tm, part],
            device_id={"tm": to},
            device_id_type=MESH,
        )

    def landed(source, part):
        rows = pl.ds(pl.multiple_of(part * sub, sub), sub)
        return pltpu.make_async_remote_copy(
            src_ref=stage.at[source, rows],
            dst_ref=land.at[source, rows],
            send_sem=a2a_send.at[source, part],
            recv_sem=a2a_recv.at[source, part],
            device_id={"tm": source},
            device_id_type=MESH,
        )

    def block(part, carry):
        def rows_of(to):
            return pl.ds(pl.multiple_of(to * item + part * sub, sub), sub)

        here = pl.ds(pl.multiple_of(part * sub, sub), sub)
        summed = jnp.concatenate([acc[rows_of(to)] for to in range(n_tm)], axis=0)
        based = jnp.concatenate([root[rows_of(to)] for to in range(n_tm)], axis=0)
        combined = based + matmul(summed.astype(jnp.bfloat16), wagg_v[...])
        graph_rows = jax.nn.gelu(combined).astype(jnp.bfloat16)
        for to in range(n_tm):
            stage[to, here] = graph_rows[to * sub : (to + 1) * sub]

        def send(i, inner):
            trade(lax.rem(tm + i, n_tm), part).start()
            return inner

        lax.fori_loop(1, n_tm, send, 0)
        land[tm, here] = stage[tm, here]
        return carry

    lax.fori_loop(0, item // sub, block, 0)

    def await_rows(part):
        def one(i, inner):
            landed(lax.rem(tm + i, n_tm), part).wait_recv()
            return inner

        lax.fori_loop(1, n_tm, one, 0)

    def hand_over(part):
        rows = pl.ds(pl.multiple_of(part * sub, sub), sub)
        return pltpu.make_async_copy(out_v.at[:, rows], out_ref.at[:, rows], out_sem.at[part])

    def hand_out(part):
        hand_over(part).start()

    temporal_body(
        await_rows, sub, land, embed_ref, gain1_ref, qkv_v, wout_v, gain2_ref, up_v, down_v, out_v, hand_out
    )

    def settle_own(part, carry):
        settle(me, part, has_right, has_left)
        return carry

    lax.fori_loop(0, chunks, settle_own, 0)

    def settle_step(i, carry):
        hop = i // chunks + 1
        part = lax.rem(i, chunks)
        low = z - hop
        high = z + hop

        @pl.when(low >= 0)
        def _():
            settle(low * CORES + core, part, has_right, False)

        @pl.when(high < chips)
        def _():
            settle(high * CORES + core, part, False, has_left)

        return carry

    lax.fori_loop(0, (chips - 1) * chunks, settle_step, 0)

    def finish(i, carry):
        trade(lax.rem(tm + 1 + i // (item // sub), n_tm), lax.rem(i, item // sub)).wait_send()
        return carry

    lax.fori_loop(0, (n_tm - 1) * (item // sub), finish, 0)

    def handed(part, carry):
        hand_over(part).wait()
        return carry

    lax.fori_loop(0, item // sub, handed, 0)


def norm_rows(values, gain):
    scale = lax.rsqrt(jnp.mean(values * values, axis=-1, keepdims=True) + 1e-06)
    return values * scale * gain


def matmul(left, right):
    return jnp.dot(left, right, preferred_element_type=jnp.float32)


def temporal_body(
    await_rows, size, rows_ref, embed_ref, gain1_ref, qkv_ref, wout_ref, gain2_ref, up_ref, down_ref, out_ref, hand_out
):
    snaps, items, width = rows_ref.shape
    head = width // HEADS
    lanes = 128
    col_head = lax.broadcasted_iota(jnp.int32, (width, lanes), 0) // head
    gather_heads = (col_head == lax.broadcasted_iota(jnp.int32, (width, lanes), 1)).astype(jnp.bfloat16)
    row_head = lax.broadcasted_iota(jnp.int32, (lanes, width), 1) // head
    widen_heads = (row_head == lax.broadcasted_iota(jnp.int32, (lanes, width), 0)).astype(jnp.bfloat16)

    def body(i, carry):
        await_rows(i)
        at = pl.ds(pl.multiple_of(i * size, size), size)
        embed = embed_ref[...].astype(jnp.float32)
        mixed = jnp.concatenate(
            [rows_ref[t, at].astype(jnp.float32) + embed[t : t + 1] for t in range(snaps)], axis=0
        )
        normed = norm_rows(mixed, gain1_ref[...].astype(jnp.float32)[None]).astype(jnp.bfloat16)
        qkv = matmul(normed, qkv_ref[...]).astype(jnp.bfloat16)
        query = [qkv[t * size : (t + 1) * size, :width].astype(jnp.float32) for t in range(snaps)]
        keys = [qkv[t * size : (t + 1) * size, width : 2 * width].astype(jnp.float32) for t in range(snaps)]
        vals = [qkv[t * size : (t + 1) * size, 2 * width :].astype(jnp.float32) for t in range(snaps)]
        uppers, lowers = [], []
        for t in range(snaps):
            for u in range(t + 1):
                product = query[t] * keys[u]
                upper = product.astype(jnp.bfloat16)
                uppers.append(upper)
                lowers.append((product - upper.astype(jnp.float32)).astype(jnp.bfloat16))
        totals = matmul(jnp.concatenate(uppers + lowers, axis=0), gather_heads)
        count = len(uppers) * size
        all_scores = (totals[:count] + totals[count:]) / math.sqrt(head)
        weights = []
        for t in range(snaps):
            first = t * (t + 1) // 2
            scores = [all_scores[(first + u) * size : (first + u + 1) * size] for u in range(t + 1)]
            largest = functools.reduce(jnp.maximum, scores)
            expo = [jnp.exp(score - largest) for score in scores]
            total = functools.reduce(jnp.add, expo)
            weights += [(each / total).astype(jnp.bfloat16) for each in expo]
        wide = matmul(jnp.concatenate(weights, axis=0), widen_heads)
        contexts = []
        for t in range(snaps):
            first = t * (t + 1) // 2
            terms = [wide[(first + u) * size : (first + u + 1) * size] * vals[u] for u in range(t + 1)]
            contexts.append(functools.reduce(jnp.add, terms).astype(jnp.bfloat16))
        residual = mixed + matmul(jnp.concatenate(contexts, axis=0), wout_ref[...])
        normed_two = norm_rows(residual, gain2_ref[...].astype(jnp.float32)[None]).astype(jnp.bfloat16)
        hidden = jax.nn.gelu(matmul(normed_two, up_ref[...])).astype(jnp.bfloat16)
        out = (residual + matmul(hidden, down_ref[...])).astype(out_ref.dtype)
        for t in range(snaps):
            out_ref[t, at] = out[t * size : (t + 1) * size]
        hand_out(i)
        return carry

    lax.fori_loop(0, items // size, body, 0)


def per_device(
    features,
    tile_coord,
    tile_count,
    tile_values,
    w_agg,
    w_root,
    time_embed,
    gain_first,
    w_qkv,
    w_out,
    gain_second,
    w_up,
    w_down,
):
    own = features[0]
    pairs = tile_coord[0]
    tiles = tile_values[0]
    local, width = own.shape
    slots, tile = tiles.shape[0], tiles.shape[1]
    n_vertex = lax.axis_size("vertex")
    n_tm = lax.axis_size("tm")
    row_blocks = local // tile
    col_blocks = n_vertex * row_blocks
    chunk = 2 * tile
    chunks = local // chunk
    item = local // n_tm
    sub = max(16, min(item, 256 // n_tm))

    anywhere = pl.BlockSpec(memory_space=pl.ANY)
    vmem = pl.BlockSpec(memory_space=pltpu.VMEM)
    return pl.pallas_call(
        functools.partial(graph_kernel, (n_vertex, n_tm, chunks, chunk, tile, slots, sub)),
        out_shape=jax.ShapeDtypeStruct((n_tm, item, width), jnp.bfloat16),
        in_specs=[pl.BlockSpec(memory_space=pltpu.SMEM), vmem] + [anywhere] * 8 + [vmem] * 3,
        out_specs=anywhere,
        scratch_shapes=[
            pltpu.VMEM((n_vertex, local, width), jnp.bfloat16),
            pltpu.VMEM((slots + 1, tile, tile), jnp.bfloat16),
            pltpu.VMEM(w_agg.shape, jnp.bfloat16),
            pltpu.VMEM(w_root.shape, jnp.bfloat16),
            pltpu.VMEM(w_qkv.shape, jnp.bfloat16),
            pltpu.VMEM(w_out.shape, jnp.bfloat16),
            pltpu.VMEM(w_up.shape, jnp.bfloat16),
            pltpu.VMEM(w_down.shape, jnp.bfloat16),
            pltpu.VMEM((local, width), jnp.float32),
            pltpu.VMEM((local, width), jnp.float32),
            pltpu.VMEM((local, chunk), jnp.bfloat16),
            pltpu.VMEM((n_tm, item, width), jnp.bfloat16),
            pltpu.VMEM((n_tm, item, width), jnp.bfloat16),
            pltpu.VMEM((n_tm, item, width), jnp.bfloat16),
            pltpu.SemaphoreType.DMA((item // sub,)),
            pltpu.VMEM((row_blocks * col_blocks // LANES, LANES), jnp.int32),
            pltpu.SMEM((row_blocks * col_blocks // LANES, LANES), jnp.int32),
            pltpu.SemaphoreType.DMA((9,)),
            pltpu.SemaphoreType.DMA((3, n_vertex, chunks)),
            pltpu.SemaphoreType.DMA((n_vertex, chunks)),
            pltpu.SemaphoreType.DMA((n_tm, item // sub)),
            pltpu.SemaphoreType.DMA((n_tm, item // sub)),
        ],
        compiler_params=pltpu.CompilerParams(
            collective_id=0, has_side_effects=True, vmem_limit_bytes=56 * MIB
        ),
    )(tile_count, pairs.T, own, tiles, w_agg, w_root, w_qkv, w_out, w_up, w_down, time_embed, gain_first, gain_second)


def solution(mesh):
    return jax.shard_map(
        per_device,
        mesh=mesh,
        in_specs=(
            P("tm", "vertex", None),
            P("tm", "vertex", None),
            P("tm", "vertex"),
            P("tm", "vertex", None, None),
            P(),
            P(),
            P(),
            P(),
            P(),
            P(),
            P(),
            P(),
            P(),
        ),
        out_specs=P(None, ("vertex", "tm"), None),
        check_vma=False,
    )
```
